512 devices in a mesh: facet: 16 (over y, x_lo, core), sub: 32 (over x_hi, z).
Axes of the slice: x: 4 (x_hi: 2, x_lo: 2; x = x_hi * 2 + x_lo), y: 4, z: 16, core: 2. Of those that a mesh axis runs over, the one named last changes fastest.
Arguments:
- facet_image: bfloat16 [16, 32, 64, 16384], P('facet', 'sub'), may hold values from -6 to 6
- correction: float32 [16, 16384], P('facet'), may hold values from 0.5 to 2
- facet_sizes: int32 [16], P('facet'), may hold values from 8192 to 16384, as said below
- facet_offsets: int32 [16], P('facet'), may hold values from 0 to 262143
- counts: int32 [16], P('facet'), may hold values from 8 to 32, as said below
- sub_lists: int32 [16, 32], P('facet'), may hold values from 0 to 31, each once within a row
- sub_offsets: int32 [32], replicated, may hold values from 0 to 16383
- window: float32 [512], replicated, may hold values from 0.5 to 2
Outputs:
- subgrids: float32 [32, 2, 32, 64, 512], P('sub', None, None, 'facet')
The draws below stay inside these ranges and needn't reach their ends.
Inputs may be any that keep to these rules, and one draw needn't show every extreme that they name: `facet_sizes`: every facet has at least half of 16384 rows, and some facet has exactly 16384. Some facet contributes to all 32 subgrids; only the first counts[f] slots of a facet's list are used. `sub_lists`: each facet's list names every subgrid once.
All inputs are finite; a program needn't handle non-finite values.
Results may differ from the reference program's by a relative error of at most 0.015.
Values may be sent and summed in bfloat16 or wider, within the bound.
A program may use at most 64 MiB of HBM per device.

```python
import math
import jax
import jax.numpy as jnp
from jax import lax

P_SIZE = 16384
SPLIT = 128
SPAN = 128
XM = 512
GRID = 262144
KD = 64
FACETS = 16
SUBGRIDS = 32
COLBLK = 32


def draw_facet_sizes(key, part):
    key = jax.random.fold_in(key, 11)
    first_key, second_key = jax.random.split(key)
    sizes_drawn = jax.random.randint(first_key, (FACETS,), P_SIZE // 2, P_SIZE + 1)
    picked = jax.random.randint(second_key, (), 0, FACETS)
    return jnp.where(jnp.arange(FACETS) == picked, P_SIZE, sizes_drawn).astype(jnp.int32)


def draw_counts(key, part):
    key = jax.random.fold_in(key, 23)
    first_key, second_key = jax.random.split(key)
    raw_values = jax.random.randint(first_key, (FACETS,), 1, SUBGRIDS + 1)
    shaped = jnp.maximum(SUBGRIDS // 4, raw_values * raw_values // SUBGRIDS)
    picked = jax.random.randint(second_key, (), 0, FACETS)
    return jnp.where(jnp.arange(FACETS) == picked, SUBGRIDS, shaped).astype(jnp.int32)


def set_ends(array, key, low, top_value):
    extent = array.shape
    spot = [jax.random.randint(jax.random.fold_in(key, axis), (), 0, extent[axis]) for axis in range(len(extent))]
    array = array.at[tuple(spot)].set(low)
    longest = extent.index(max(extent))
    spot[longest] = (spot[longest] + 1) % extent[longest]
    return array.at[tuple(spot)].set(top_value)


def level_of(key, extent, cuts, smallest, largest):
    def one(axis_at, parts):
        steps = jax.random.uniform(jax.random.fold_in(jax.random.fold_in(key, 6), axis_at), (parts,), jnp.float32, smallest / len(cuts), largest / len(cuts))
        return jnp.repeat(jnp.exp(steps), extent[axis_at] // parts).reshape((-1,) + (1,) * (len(extent) - axis_at - 1))

    factor_of = one(*cuts[0])
    for cut in cuts[1:]:
        factor_of = factor_of * one(*cut)
    return factor_of


def gaussian(key, extent, width, most, cuts=(), kind=jnp.bfloat16):
    gain = level_of(key, extent, cuts, -0.22, 0.18) if cuts else 1.0
    values = jax.random.normal(key, extent, jnp.float32) * width * gain
    return jnp.minimum(jnp.maximum(values, -most), most).astype(kind)


def setup_inputs(seed: int = 0) -> dict:
    key_of = jax.random.split(jax.random.key(seed), 9)
    return {
        "facet_image": gaussian(key_of[0], (FACETS, COLBLK, KD, P_SIZE), 1.0, 6.0, ((0, 16), (1, 32))),
        "correction": jnp.clip(jnp.exp(math.log(2.0) - 1.3862944 * jax.random.uniform(key_of[1], (FACETS, P_SIZE), jnp.float32) ** level_of(key_of[1], (FACETS, P_SIZE), ((0, 16),), -0.2, 0.2)), 0.5, 2.0),
        "facet_sizes": draw_facet_sizes(jax.random.fold_in(key_of[8], 71), 0),
        "facet_offsets": set_ends(jax.random.randint(key_of[3], (FACETS,), 0, GRID), jax.random.fold_in(key_of[3], 1), 0, GRID - 1).astype(jnp.int32),
        "counts": draw_counts(jax.random.fold_in(key_of[8], 71), 0),
        "sub_lists": jax.vmap(lambda own: jax.random.permutation(own, SUBGRIDS))(jax.random.split(key_of[5], FACETS)).reshape((FACETS, SUBGRIDS)).astype(jnp.int32),
        "sub_offsets": set_ends(jax.random.randint(key_of[6], (SUBGRIDS,), 0, P_SIZE), jax.random.fold_in(key_of[6], 1), 0, P_SIZE - 1).astype(jnp.int32),
        "window": jnp.clip(jnp.exp(jax.random.uniform(key_of[7], (XM,), jnp.float32, math.log(0.5), math.log(2.0))), 0.5, 2.0),
    }


def cos_sin(count_left, count_right, period, factor):
    left_ids = jnp.arange(count_left, dtype=jnp.int32)[:, None]
    right_ids = jnp.arange(count_right, dtype=jnp.int32)[None, :]
    phase_angle = (left_ids * right_ids % period).astype(jnp.float32) * (2.0 * math.pi / period)
    return (jnp.cos(phase_angle) * factor, jnp.sin(phase_angle) * factor)

def make_tables():
    cos_one, sin_one = cos_sin(SPLIT, SPLIT, SPLIT, 1.0 / math.sqrt(SPLIT))
    table_one = jnp.concatenate([cos_one, -sin_one], axis=0).astype(jnp.bfloat16)
    turn_cos, turn_sin = cos_sin(SPLIT, SPAN, P_SIZE, 1.0)
    cos_two, sin_two = cos_sin(SPAN, SPAN, SPAN, 1.0 / math.sqrt(SPAN))
    upper_two = jnp.concatenate([cos_two, -sin_two], axis=1)
    lower_two = jnp.concatenate([sin_two, cos_two], axis=1)
    table_two = jnp.concatenate([upper_two, lower_two], axis=0).astype(jnp.bfloat16)
    cos_three, sin_three = cos_sin(XM, XM, XM, 1.0 / math.sqrt(XM))
    upper_three = jnp.stack([cos_three, sin_three], axis=1)
    lower_three = jnp.stack([-sin_three, cos_three], axis=1)
    table_three = jnp.concatenate([upper_three, lower_three], axis=0).astype(jnp.bfloat16)
    return (table_one, turn_cos, turn_sin, table_two, table_three)

def prepare(columns, gains, limit, tables):
    table_one, turn_cos, turn_sin, table_two, table_three = tables
    column_count = columns.shape[0]
    positions = jnp.arange(P_SIZE, dtype=jnp.int32)
    masked = jnp.where(positions[None, :] < limit, columns.astype(jnp.float32) * gains[None, :], 0.0).astype(jnp.bfloat16)
    split_rows = masked.reshape(column_count, SPLIT, SPAN)
    section_one = jnp.einsum('ra,kab->krb', table_one.astype(jnp.float32), split_rows.astype(jnp.float32), precision=lax.Precision.HIGHEST)
    real_part = section_one[:, :SPLIT]
    imag_part = section_one[:, SPLIT:]
    turned = jnp.concatenate([real_part * turn_cos + imag_part * turn_sin, imag_part * turn_cos - real_part * turn_sin], axis=2).astype(jnp.bfloat16)
    spectrum = jnp.einsum('kut,tw->kuw', turned.astype(jnp.float32), table_two.astype(jnp.float32), precision=lax.Precision.HIGHEST).astype(jnp.bfloat16)
    return spectrum.reshape(column_count, SPLIT, 2, SPAN).transpose(0, 2, 3, 1).reshape(column_count, 2, P_SIZE)

def extract(prepared, shifts, offset, window, table_three):
    extended = jnp.concatenate([prepared, prepared[:, :, :XM]], axis=2)
    pieces = jax.vmap(lambda shift_one: lax.dynamic_slice_in_dim(extended, shift_one, XM, axis=2))(shifts)
    freqs = (shifts[:, None] + jnp.arange(XM, dtype=jnp.int32)[None, :]) % P_SIZE
    turns = freqs * (offset % P_SIZE) % P_SIZE
    phase_angle = turns.astype(jnp.float32) * (2.0 * math.pi / P_SIZE)
    cosine = jnp.cos(phase_angle)[:, None, :]
    sine = jnp.sin(phase_angle)[:, None, :]
    real_part = pieces[:, :, 0].astype(jnp.float32)
    imag_part = pieces[:, :, 1].astype(jnp.float32)
    spectrum = jnp.concatenate([window * (real_part * cosine + imag_part * sine), window * (imag_part * cosine - real_part * sine)], axis=2).astype(jnp.bfloat16)
    result = jnp.einsum('lkt,thm->lhkm', spectrum.astype(jnp.float32), table_three.astype(jnp.float32), precision=lax.Precision.HIGHEST)
    return result.astype(jnp.bfloat16)

def reference(facet_image, correction, facet_sizes, facet_offsets, counts, sub_lists, sub_offsets, window):
    tables = make_tables()
    column_total = COLBLK * KD
    subgrid_ids = jnp.arange(SUBGRIDS, dtype=jnp.int32)
    total = jnp.zeros((SUBGRIDS, 2, column_total, XM), jnp.float32)
    for owner in range(FACETS):
        columns = facet_image[owner].reshape(column_total, P_SIZE)
        prepared = prepare(columns, correction[owner], facet_sizes[owner], tables)
        chosen = sub_lists[owner]
        shifts = sub_offsets[chosen].astype(jnp.int32)
        contribution = extract(prepared, shifts, facet_offsets[owner], window, tables[4])
        live = subgrid_ids < counts[owner]
        selector = ((chosen[:, None] == subgrid_ids[None, :]) & live[:, None]).astype(jnp.float32)
        total = total + jnp.einsum('lg,lhkm->ghkm', selector, contribution.astype(jnp.float32), precision=lax.Precision.HIGHEST)
    return total.reshape(SUBGRIDS, 2, COLBLK, KD, XM)
```

```python
import functools
import math

import jax
import jax.numpy as jnp
import ml_dtypes
import numpy as np
from jax import lax
from jax.experimental import pallas as pl
from jax.experimental.pallas import tpu as pltpu
from jax.sharding import PartitionSpec as P

N = 16384
XM = 512
KD = 64
SUBS = 32
GROUPS = 2
PER = SUBS // GROUPS
CHUNKS = 2 * GROUPS
ROWS = PER * 16
F32 = jnp.float32
BF16 = jnp.bfloat16
MESH = pl.DeviceIdType.MESH


def table_one():
    turns = np.outer(np.arange(128), np.arange(128)) % 128 * (2.0 * np.pi / 128)
    table = np.concatenate([np.cos(turns), -np.sin(turns)], axis=0) / math.sqrt(128.0)
    return table.astype(np.float32).astype(ml_dtypes.bfloat16)


def table_three():
    turns = np.outer(np.arange(XM), np.arange(XM)) % XM * (2.0 * np.pi / XM)
    cosine, sine = np.cos(turns), np.sin(turns)
    table = np.block([[cosine, sine], [-sine, cosine]]) / math.sqrt(XM)
    return table.astype(np.float32).astype(ml_dtypes.bfloat16)


def cos_turn(index):
    index = index & (N - 1)
    quarter = (index + 2048) >> 12
    angle = (index - (quarter << 12)).astype(F32) * (2.0 * math.pi / N)
    square = angle * angle
    even = 1.0 + square * (-0.5 + square * (1 / 24 + square * (-1 / 720 + square * (1 / 40320))))
    odd = angle * (1.0 + square * (-1 / 6 + square * (1 / 120 + square * (-1 / 5040))))
    value = jnp.where((quarter & 1) == 1, odd, even)
    return jnp.where(((quarter + 1) & 2) == 2, -value, value)


def iota(shape, axis):
    return lax.broadcasted_iota(jnp.int32, shape, axis)


def add_to(target, *others):
    def body(i, carry):
        rows = pl.ds(pl.multiple_of(i * 64, 64), 64)
        total = target[rows, :].astype(F32)
        for other in others:
            total = total + other[rows, :].astype(F32)
        target[rows, :] = total.astype(BF16)
        return carry

    lax.fori_loop(0, ROWS // 64, body, 0)


def kernel(
    image_hbm, gain_ref, size_ref, offset_ref, count_ref, starts_ref, list_ref, window_ref, one_ref, three_hbm,
    out_ref,
    image, three, plane, two, turn_cos, turn_sin, live, spec, parts, core_in, up_in, down_in, up_two, down_two,
    side_in, landed, scaled,
    image_sem, three_sem, core_send, core_recv, y_send, y_recv, x_send, x_recv, sub_send, sub_recv,
):
    f, s = lax.axis_index("facet"), lax.axis_index("sub")
    core, side, y = f % 2, (f // 2) % 2, f // 4
    core_peer = f + 1 - 2 * core
    side_peer = f + 2 - 4 * side
    up = ((y + 1) % 4) * 4 + f % 4
    down = ((y + 3) % 4) * 4 + f % 4

    loads = [
        pltpu.make_async_copy(
            image_hbm.at[:, pl.ds(part * 4096, 4096)], image.at[:, pl.ds(part * 4096, 4096)], image_sem.at[part]
        )
        for part in range(4)
    ]
    for load in loads:
        load.start()
    load_three = pltpu.make_async_copy(three_hbm, three, three_sem)
    load_three.start()

    barrier = pltpu.get_barrier_semaphore()
    for peer in (core_peer, side_peer, up, down):
        pl.semaphore_signal(barrier, inc=1, device_id={"facet": peer}, device_id_type=MESH)
    for step in range(1, SUBS):
        pl.semaphore_signal(barrier, inc=1, device_id={"sub": (s + step) % SUBS}, device_id_type=MESH)

    offset = offset_ref[0] & (N - 1)
    row, lane = iota((256, 256), 0), iota((256, 256), 1)
    freq = (row >> 3) * 4 + (row & 3)
    turns = freq * ((lane & 127) + offset) * 128 + 4096 * (((row >> 2) & 1) - (lane >> 7))
    two[...] = (cos_turn(turns) * (1.0 / math.sqrt(128.0))).astype(BF16)
    turns = iota((128, 128), 0) * (iota((128, 128), 1) + offset)
    turn_cos[...] = cos_turn(turns)
    turn_sin[...] = cos_turn(turns - 4096)
    named = (list_ref[...] == iota((SUBS, SUBS), 0)) & (iota((SUBS, SUBS), 1) < count_ref[0])
    live[...] = jnp.broadcast_to(jnp.sum(jnp.where(named, 1.0, 0.0), axis=1, keepdims=True), (SUBS, 128))

    size = size_ref[0]

    def fill(a, carry):
        first = pl.multiple_of(a * 128, 128)
        gain = jnp.where(iota((1, 128), 1) + first < size, gain_ref[:, pl.ds(first, 128)], 0.0)
        plane[pl.ds(pl.multiple_of(a * KD, KD), KD), :] = image[:, pl.ds(first, 128)].astype(F32) * gain
        return carry

    for part in range(4):
        loads[part].wait()
        lax.fori_loop(part * 32, part * 32 + 32, fill, 0, unroll=2)

    def transform(half, four):
        first = 4 * four + 2 * half
        columns = [plane[pl.ds(first + j, 128, stride=KD), :] for j in range(2)]
        section = jnp.dot(
            one_ref[...], jnp.concatenate(columns, axis=1).astype(BF16), preferred_element_type=F32
        )
        turned = []
        for j in range(2):
            re, im = section[:128, j * 128 : j * 128 + 128], section[128:, j * 128 : j * 128 + 128]
            cosine, sine = turn_cos[...], turn_sin[...]
            turned.append(
                jnp.concatenate([re * cosine + im * sine, im * cosine - re * sine], axis=1).astype(BF16)
            )
        result = lax.dot_general(
            two[...], jnp.concatenate(turned, axis=0), (((1,), (1,)), ((), ())), preferred_element_type=F32
        )
        for j in range(2):
            spec[half, four, j] = result[:, j * 128 : j * 128 + 128].reshape(32, 8, 128)

    def transforms(half, begin, end):
        def body(i, carry):
            transform(half, 2 * i)
            transform(half, 2 * i + 1)
            return carry

        lax.fori_loop(begin // 2, end // 2, body, 0)

    place = (iota((8, 128), 0) & 3) * 128 + iota((8, 128), 1)

    def extract(n):
        half, group = n // GROUPS, n % GROUPS

        def body(i, carry):
            g = i * GROUPS + group
            start = starts_ref[g]
            low = (start >> 9) & 31
            inside = place >= (start & 511)
            high = (low + 1) & 31
            weight = jnp.broadcast_to(live[pl.ds(g, 1), :], (8, 128))
            rows = pl.ds(pl.multiple_of(i * 16, 16), 16)
            for four in range(16):
                pair = [
                    jnp.where(inside, spec[half, four, j, low], spec[half, four, j, high]) * weight
                    for j in range(2)
                ]
                parts[n, four % 2, four // 4, (four // 2) % 2, rows, :] = jnp.concatenate(pair, axis=0).astype(BF16)
            return carry

        lax.fori_loop(0, PER, body, 0)

    def remote(source, target, send, recv, device):
        return pltpu.make_async_remote_copy(
            src_ref=source, dst_ref=target, send_sem=send, recv_sem=recv, device_id=device, device_id_type=MESH
        )

    started = []

    def go(copy):
        copy.start()
        started.append(copy)
        return copy

    opposite, above, below = (y + 2) % 4, (y + 1) % 4, (y + 3) % 4

    def core_start(n):
        return go(remote(parts.at[n, 1 - core], core_in.at[n], core_send.at[n], core_recv.at[n], {"facet": core_peer}))

    def first_start(n, core_copy):
        core_copy.wait_recv()
        mine = parts.at[n, core]

        def add(block, x):
            add_to(mine.at[block, x], core_in.at[n, block, x])

        def send(i, block, x, target, peer):
            return go(remote(mine.at[block, x], target, y_send.at[n, i], y_recv.at[n, i], {"facet": peer}))

        copies = [None] * 6
        add(opposite, 0)
        copies[0] = send(0, opposite, 0, up_in.at[n], up)
        add(opposite, 1)
        copies[1] = send(1, opposite, 1, down_in.at[n], down)
        add(above, 1)
        copies[2] = send(2, above, 1, up_two.at[n, 1], up)
        add(below, 0)
        copies[3] = send(3, below, 0, down_two.at[n, 0], down)
        add(above, 0)
        add(below, 1)
        add(y, 0)
        add(y, 1)
        return copies

    def second_start(n, copies):
        mine = parts.at[n, core]
        copies[0].wait_recv()
        add_to(mine.at[above, 0], up_in.at[n])
        copies[4] = go(
            remote(mine.at[above, 0], up_two.at[n, 0], y_send.at[n, 4], y_recv.at[n, 4], {"facet": up})
        )
        copies[1].wait_recv()
        add_to(mine.at[below, 1], down_in.at[n])
        copies[5] = go(
            remote(mine.at[below, 1], down_two.at[n, 1], y_send.at[n, 5], y_recv.at[n, 5], {"facet": down})
        )
        return copies

    def side_start(n, copies):
        mine = parts.at[n, core, y]
        for i in range(2, 6):
            copies[i].wait_recv()
        add_to(mine.at[1 - side], up_two.at[n, 1 - side], down_two.at[n, 1 - side])
        copy = go(remote(mine.at[1 - side], side_in.at[n], x_send.at[n], x_recv.at[n], {"facet": side_peer}))
        add_to(mine.at[side], up_two.at[n, side], down_two.at[n, side])
        return copy

    def sub_start(n, side_copy):
        half, group = n // GROUPS, n % GROUPS
        mine = parts.at[n, core, y, side]
        side_copy.wait_recv()
        add_to(mine, side_in.at[n])
        home = s // GROUPS
        for step in sorted(range(PER), key=lambda d: -min(d, PER - d)):
            i = (home + step) % PER
            block = mine.at[pl.ds(pl.multiple_of(i * 16, 16), 16), :]
            copy = remote(
                block, landed.at[half, s], sub_send.at[n], sub_recv.at[half], {"sub": i * GROUPS + group}
            )
            if step:
                copy.start()
            else:
                own = s % GROUPS == group

                @pl.when(own)
                def _():
                    landed[half, s] = block[...]

                @pl.when(jnp.logical_not(own))
                def _():
                    copy.start()

    transforms(0, 0, 16)
    core_copies, y_copies, side_copies = {}, {}, {}
    for step in range(CHUNKS + 4):
        if 0 <= step - 4 < CHUNKS:
            sub_start(step - 4, side_copies[step - 4])
        if 0 <= step - 3 < CHUNKS:
            side_copies[step - 3] = side_start(step - 3, y_copies[step - 3])
        if 0 <= step - 2 < CHUNKS:
            second_start(step - 2, y_copies[step - 2])
        if 0 <= step - 1 < CHUNKS:
            y_copies[step - 1] = first_start(step - 1, core_copies[step - 1])
        if step < CHUNKS:
            extract(step)
            if step == 0:
                pl.semaphore_wait(barrier, SUBS + 3)
            core_copies[step] = core_start(step)
        if step < GROUPS:
            transforms(1, step * (16 // GROUPS), (step + 1) * (16 // GROUPS))

    start = starts_ref[s]
    within = start & 511
    shift, blocks = within & 127, within >> 7
    turned_window = window_ref[...]
    for bit in range(7):
        turned_window = jnp.where(
            ((shift >> bit) & 1) == 1, pltpu.roll(turned_window, 1 << bit, 1), turned_window
        )
    block_of, lane_of = iota((8, 128), 0), iota((8, 128), 1)
    taken = (block_of - blocks - jnp.where(lane_of < shift, 1, 0)) & 3
    weight = jnp.zeros((8, 128), F32)
    for b in range(4):
        weight = jnp.where(taken == b, jnp.broadcast_to(turned_window[b : b + 1, :], (8, 128)), weight)
    weight = jnp.concatenate([weight, weight], axis=0)
    turns = ((iota((1, XM), 1) * within) & 511) * 32
    back_cos, back_sin = cos_turn(turns), cos_turn(turns - 4096)

    load_three.wait()
    for half in range(2):
        got = landed.at[half, pl.ds(0, SUBS - 1)]
        pltpu.make_async_copy(got, got, sub_recv.at[half]).wait()
    for half in range(2):
        for b in range(SUBS):
            scaled[pl.ds(b * 32 + half * 16, 16), :] = landed[half, b].astype(F32) * weight
    spectrum = jnp.concatenate(
        [scaled[pl.ds(i, 128, stride=8), :].astype(BF16) for i in range(8)], axis=1
    )
    result = jnp.dot(spectrum, three[...], preferred_element_type=F32)
    re, im = result[:, :XM], result[:, XM:]
    for h, value in enumerate((re * back_cos + im * back_sin, im * back_cos - re * back_sin)):
        for b in range(SUBS):
            out_ref[h, b] = value[4 * b : 4 * b + 4, :]

    for copy in started:
        copy.wait_send()
    for n in range(CHUNKS):
        own = s % GROUPS == n % GROUPS
        sent = parts.at[n, core, y, side]

        @pl.when(own)
        def _():
            some = sent.at[pl.ds(0, ROWS - 16), :]
            pltpu.make_async_copy(some, some, sub_send.at[n]).wait()

        @pl.when(jnp.logical_not(own))
        def _():
            pltpu.make_async_copy(sent, sent, sub_send.at[n]).wait()


def local(image, correction, sizes, offsets, counts, lists, starts, window):
    vmem, smem, anywhere = (pl.BlockSpec(memory_space=m) for m in (pltpu.VMEM, pltpu.SMEM, pl.ANY))
    block = (CHUNKS, ROWS, 128)
    out = pl.pallas_call(
        kernel,
        out_shape=jax.ShapeDtypeStruct((2, SUBS, 4, XM), F32),
        in_specs=[anywhere, vmem, smem, smem, smem, smem, vmem, vmem, vmem, anywhere],
        out_specs=vmem,
        scratch_shapes=[
            pltpu.VMEM((KD, N), BF16),
            pltpu.VMEM((1024, 1024), BF16),
            pltpu.VMEM((128 * KD, 128), F32),
            pltpu.VMEM((256, 256), BF16),
            pltpu.VMEM((128, 128), F32),
            pltpu.VMEM((128, 128), F32),
            pltpu.VMEM((SUBS, 128), F32),
            pltpu.VMEM((2, 16, 2, 32, 8, 128), F32),
            pltpu.VMEM((CHUNKS, 2, 4, 2, ROWS, 128), BF16),
            pltpu.VMEM((CHUNKS, 4, 2, ROWS, 128), BF16),
            pltpu.VMEM(block, BF16),
            pltpu.VMEM(block, BF16),
            pltpu.VMEM((CHUNKS, 2, ROWS, 128), BF16),
            pltpu.VMEM((CHUNKS, 2, ROWS, 128), BF16),
            pltpu.VMEM(block, BF16),
            pltpu.VMEM((2, SUBS, 16, 128), BF16),
            pltpu.VMEM((SUBS * 32, 128), F32),
            pltpu.SemaphoreType.DMA((4,)),
            pltpu.SemaphoreType.DMA,
            pltpu.SemaphoreType.DMA((CHUNKS,)),
            pltpu.SemaphoreType.DMA((CHUNKS,)),
            pltpu.SemaphoreType.DMA((CHUNKS, 6)),
            pltpu.SemaphoreType.DMA((CHUNKS, 6)),
            pltpu.SemaphoreType.DMA((CHUNKS,)),
            pltpu.SemaphoreType.DMA((CHUNKS,)),
            pltpu.SemaphoreType.DMA((CHUNKS,)),
            pltpu.SemaphoreType.DMA((2,)),
        ],
        compiler_params=pltpu.CompilerParams(
            collective_id=0, has_side_effects=True, vmem_limit_bytes=48 * 1024 * 1024
        ),
    )(
        image.reshape(KD, N), correction, sizes, offsets, counts, starts, lists, window.reshape(4, 128),
        jnp.asarray(table_one()), jnp.asarray(table_three()),
    )
    return out.reshape(1, 2, SUBS, 4, XM)


def solution(mesh):
    in_specs = (
        P("facet", "sub", None, None),
        P("facet", None),
        P("facet"),
        P("facet"),
        P("facet"),
        P("facet", None),
        P(),
        P(),
    )
    out_specs = P("sub", None, None, "facet", None)
    return jax.shard_map(local, mesh=mesh, in_specs=in_specs, out_specs=out_specs, check_vma=False)
```

```python
import functools
import math

import jax
import jax.numpy as jnp
import ml_dtypes
import numpy as np
from jax import lax
from jax.experimental import pallas as pl
from jax.experimental.pallas import tpu as pltpu
from jax.sharding import PartitionSpec as P

N = 16384
XM = 512
KD = 64
SUBS = 32
GROUPS = 8
PER = SUBS // GROUPS
ROWS = PER * 32
HALF = ROWS // 2
ACROSS = (True, False, False, True, False, False, True, False)
ORDER = (
    ("T", 0), ("E", 0, 4), ("E", 0, 0), ("E", 0, 1), ("E", 0, 7), ("E", 0, 3), ("E", 0, 6), ("T", 1), ("E", 1, 6),
    ("E", 1, 2), ("E", 0, 2), ("S", 0, 0), ("E", 1, 0), ("E", 1, 3), ("E", 1, 1), ("A", 1), ("E", 0, 5), ("S", 0, 3),
    ("T", 2), ("E", 2, 1), ("B", 1), ("E", 2, 0), ("E", 2, 3), ("E", 2, 2), ("A", 2), ("B", 2), ("S", 1, 0),
    ("A", 0), ("T", 3), ("S", 1, 3), ("E", 3, 1), ("E", 3, 0), ("S", 2, 0), ("B", 0), ("E", 3, 4), ("E", 3, 5),
    ("E", 1, 4), ("O", 1), ("A", 4), ("A", 3), ("S", 2, 3), ("E", 3, 3), ("E", 2, 6), ("B", 3), ("E", 3, 7),
    ("E", 2, 4), ("B", 4), ("E", 1, 5), ("A", 5), ("E", 3, 6), ("E", 3, 2), ("E", 2, 5), ("B", 5), ("S", 3, 0),
    ("S", 0, 6), ("E", 2, 7), ("B", 7), ("L", 1), ("S", 1, 6), ("E", 1, 7), ("A", 7), ("O", 2), ("S", 3, 3),
    ("O", 0), ("S", 2, 6), ("O", 3), ("O", 4), ("S", 3, 6), ("L", 2), ("O", 5), ("A", 6), ("B", 6), ("L", 4),
    ("O", 7), ("L", 5), ("O", 6), ("L", 7),
)
F32 = jnp.float32
BF16 = jnp.bfloat16
MESH = pl.DeviceIdType.MESH


def table_one():
    turns = np.outer(np.arange(128), np.arange(128)) % 128 * (2.0 * np.pi / 128)
    table = np.concatenate([np.cos(turns), -np.sin(turns)], axis=0) / math.sqrt(128.0)
    return table.astype(np.float32).astype(ml_dtypes.bfloat16)


def table_three():
    turns = np.outer(np.arange(XM), np.arange(XM)) % XM * (2.0 * np.pi / XM)
    table = np.concatenate([np.cos(turns), np.sin(turns)], axis=1) / math.sqrt(XM)
    return table.astype(np.float32).astype(ml_dtypes.bfloat16)


def cos_turn(index):
    index = index & (N - 1)
    quarter = (index + 2048) >> 12
    angle = (index - (quarter << 12)).astype(F32) * (2.0 * math.pi / N)
    square = angle * angle
    even = 1.0 + square * (-0.5 + square * (1 / 24 + square * (-1 / 720 + square * (1 / 40320))))
    odd = angle * (1.0 + square * (-1 / 6 + square * (1 / 120 + square * (-1 / 5040))))
    value = jnp.where((quarter & 1) == 1, odd, even)
    return jnp.where(((quarter + 1) & 2) == 2, -value, value)


def iota(shape, axis):
    return lax.broadcasted_iota(jnp.int32, shape, axis)


def add_to(target, *others):
    count = target.shape[0]
    size = max(size for size in (16, 32, 48, 64, 80, 96, 128) if count % size == 0)

    def body(i, carry):
        rows = pl.ds(pl.multiple_of(i * size, size), size)
        total = target[rows, :].astype(F32)
        for other in others:
            total = total + other[rows, :].astype(F32)
        target[rows, :] = total.astype(BF16)
        return carry

    lax.fori_loop(0, count // size, body, 0)


def kernel(
    image_hbm, gain_hbm, size_hbm, offset_hbm, count_hbm, starts_hbm, list_hbm, window_hbm, one_hbm, three_hbm,
    out_ref,
    gain_ref, size_ref, offset_ref, count_ref, starts_ref, list_ref, window_ref, one_ref,
    image, three, plane, two, turn, live, given, taken, spec, parts, side_in, up_in, down_in, up_two, down_two,
    landed, scaled,
    small_sem, image_sem, three_sem, table_sem, given_sem, side_sem, y_sem, sub_send_sem, sub_recv_sem,
):
    f, s = lax.axis_index("facet"), lax.axis_index("sub")
    core, side, y = f % 2, (f // 2) % 2, f // 4
    core_peer = f + 1 - 2 * core
    side_peer = f + 2 - 4 * side
    up = ((y + 1) % 4) * 4 + f % 4
    down = ((y + 3) % 4) * 4 + f % 4

    small = [
        pltpu.make_async_copy(source, target, small_sem.at[i])
        for i, (source, target) in enumerate(
            (
                (offset_hbm, offset_ref), (count_hbm, count_ref), (list_hbm, list_ref), (size_hbm, size_ref), (gain_hbm, gain_ref), (one_hbm, one_ref),
                (starts_hbm, starts_ref), (window_hbm, window_ref),
            )
        )
    ]
    for load in small:
        load.start()
    loads = [
        pltpu.make_async_copy(
            image_hbm.at[:, pl.ds(part * 4096, 4096)], image.at[:, pl.ds(part * 4096, 4096)], image_sem.at[part]
        )
        for part in range(4)
    ]
    for load in loads:
        load.start()
    load_three = pltpu.make_async_copy(three_hbm, three, three_sem)
    load_three.start()

    barrier = pltpu.get_barrier_semaphore()
    for peer in (core_peer, side_peer, up, down):
        pl.semaphore_signal(barrier, inc=1, device_id={"facet": peer}, device_id_type=MESH)
    for step in range(1, SUBS):
        pl.semaphore_signal(barrier, inc=1, device_id={"sub": (s + step) % SUBS}, device_id_type=MESH)

    for load in small:
        load.wait()
    offset = offset_ref[0] & (N - 1)
    row, lane = iota((256, 256), 0), iota((256, 256), 1)
    freq = (row >> 3) * 4 + (row & 3)
    turns = freq * ((lane & 127) + offset) * 128 + 4096 * (((row >> 2) & 1) - (lane >> 7))
    two[0] = (cos_turn(turns) * (1.0 / math.sqrt(128.0))).astype(BF16)
    turns = iota((128, 128), 0) * (iota((128, 128), 1) + offset)
    turn[0, 0] = cos_turn(turns)
    turn[0, 1] = cos_turn(turns - 4096)
    named = (list_ref[...] == iota((SUBS, SUBS), 0)) & (iota((SUBS, SUBS), 1) < count_ref[0])
    live[0] = jnp.broadcast_to(jnp.sum(jnp.where(named, 1.0, 0.0), axis=1, keepdims=True), (SUBS, 128))

    started = []

    def go(source, target, send, recv, device):
        copy = pltpu.make_async_remote_copy(
            src_ref=source, dst_ref=target, send_sem=send, recv_sem=recv, device_id=device, device_id_type=MESH
        )
        copy.start()
        started.append(copy)
        return copy

    size = size_ref[0]

    def fill(a, carry):
        first = pl.multiple_of(a * 128, 128)
        gain = jnp.where(iota((1, 128), 1) + first < size, gain_ref[:, pl.ds(first, 128)], 0.0)
        plane[pl.ds(pl.multiple_of(a * KD, KD), KD), :] = image[:, pl.ds(first, 128)].astype(F32) * gain
        return carry

    for part in range(4):
        loads[part].wait()
        lax.fori_loop(part * 32, part * 32 + 32, fill, 0, unroll=2)

    block_y = ((y + 2) % 4, (y + 1) % 4, (y + 3) % 4, y)

    for q in range(4):
        for x in range(2):
            for j in range(4):
                column = 16 * block_y[q] + 8 * x + 4 * (1 - core) + j
                given[q, 4 * x + j] = plane[pl.ds(column, 128, stride=KD), :].astype(BF16)

    pl.semaphore_wait(barrier, SUBS + 3)
    tables = [
        go(table.at[0], table.at[1], table_sem.at[0, i], table_sem.at[1, i], {"facet": core_peer})
        for i, table in enumerate((two, turn, live))
    ]

    gifts = [
        go(given.at[q], taken.at[q], given_sem.at[0, q], given_sem.at[1, q], {"facet": core_peer}) for q in range(4)
    ]

    def transform(q, source, pair):
        if source == 0:
            first = 16 * block_y[q] + 8 * (pair // 2) + 4 * core + 2 * (pair % 2)
            columns = [plane[pl.ds(first + j, 128, stride=KD), :].astype(BF16) for j in range(2)]
        else:
            columns = [taken[q, 2 * pair + j] for j in range(2)]
        section = jnp.dot(one_ref[...], jnp.concatenate(columns, axis=1), preferred_element_type=F32)
        turned = []
        for j in range(2):
            re, im = section[:128, j * 128 : j * 128 + 128], section[128:, j * 128 : j * 128 + 128]
            cosine, sine = turn[source, 0], turn[source, 1]
            turned.append(
                jnp.concatenate([re * cosine + im * sine, im * cosine - re * sine], axis=1).astype(BF16)
            )
        result = lax.dot_general(
            two[source], jnp.concatenate(turned, axis=0), (((1,), (1,)), ((), ())), preferred_element_type=F32
        )
        for j in range(2):
            spec[q, source, pair, j] = result[:, j * 128 : j * 128 + 128].reshape(32, 8, 128)

    def transforms(q):
        if q > 0:
            gifts[q].wait_recv()
        for pair in range(4):
            transform(q, 0, pair)
        if q == 0:
            for table in tables:
                table.wait_recv()
            gifts[q].wait_recv()
        for pair in range(4):
            transform(q, 1, pair)

    place = (iota((8, 128), 0) & 3) * 128 + iota((8, 128), 1)

    def extract(q, m):
        def body(i, carry):
            g = i * GROUPS + m
            start = starts_ref[g]
            low = (start >> 9) & 31
            high = (low + 1) & 31
            inside = place >= (start & 511)
            weights = [jnp.broadcast_to(live[source, pl.ds(g, 1), :], (8, 128)) for source in range(2)]
            for pair in range(4):
                tiles = []
                for j in range(2):
                    windows = [
                        jnp.where(inside, spec[q, source, pair, j, low], spec[q, source, pair, j, high])
                        for source in range(2)
                    ]
                    tiles.append(windows[0] * weights[0] + windows[1] * weights[1])
                rows = pl.ds(pl.multiple_of(m * ROWS + i * 32 + (pair % 2) * 16, 16), 16)
                parts[q, pair // 2, rows, :] = jnp.concatenate(tiles, axis=0).astype(BF16)
            return carry

        lax.fori_loop(0, PER, body, 0, unroll=2)

    copies = {}

    def group(m):
        return pl.ds(m * ROWS, ROWS)

    def side_send(q, m):
        copies["side", q, m] = go(
            parts.at[q, 1 - side, group(m)], side_in.at[m, q],
            side_sem.at[0, q, m], side_sem.at[1, q, m], {"facet": side_peer},
        )

    def side_add(q, m):
        copies["side", q, m].wait_recv()
        add_to(parts.at[q, side, group(m)], side_in.at[m, q])

    def piece(q, m, p):
        if ACROSS[m]:
            return parts.at[q, side, pl.ds(m * ROWS + p * HALF, HALF)]
        return parts.at[q, p, group(m)]

    size_of = [pl.ds(0, HALF if across else ROWS) for across in ACROSS]

    def along_y(number, q, m, p, target, peer):
        copies["y", number, m] = go(
            piece(q, m, p), target, y_sem.at[0, number, m], y_sem.at[1, number, m], {"facet": peer}
        )

    def opposite_send(m):
        along_y(0, 0, m, 0, up_in.at[m, size_of[m]], up)
        along_y(1, 0, m, 1, down_in.at[m, size_of[m]], down)

    def above_send(m):
        along_y(2, 1, m, 1, up_two.at[m, 1, size_of[m]], up)

    def above_pass(m):
        copies["y", 0, m].wait_recv()
        add_to(piece(1, m, 0), up_in.at[m, size_of[m]])
        along_y(3, 1, m, 0, up_two.at[m, 0, size_of[m]], up)

    def below_send(m):
        along_y(4, 2, m, 0, down_two.at[m, 0, size_of[m]], down)

    def below_pass(m):
        copies["y", 1, m].wait_recv()
        add_to(piece(2, m, 1), down_in.at[m, size_of[m]])
        along_y(5, 2, m, 1, down_two.at[m, 1, size_of[m]], down)

    def own_add(m):
        for number in range(2, 6):
            copies["y", number, m].wait_recv()
        for p in range(2):
            add_to(piece(3, m, p), up_two.at[m, p, size_of[m]], down_two.at[m, p, size_of[m]])

    def sub_send(m):
        mine = parts.at[3, side]
        home = s // GROUPS
        for step in sorted(range(PER), key=lambda d: -min(d, PER - d)):
            i = (home + step) % PER
            block = mine.at[pl.ds(pl.multiple_of(m * ROWS + i * 32, 32), 32), :]
            copy = pltpu.make_async_remote_copy(
                src_ref=block, dst_ref=landed.at[s], send_sem=sub_send_sem.at[m], recv_sem=sub_recv_sem,
                device_id={"sub": i * GROUPS + m}, device_id_type=MESH,
            )
            if step:
                copy.start()
            else:
                own = s % GROUPS == m

                @pl.when(own)
                def _():
                    landed[s] = block[...]

                @pl.when(jnp.logical_not(own))
                def _():
                    copy.start()

    sends = (opposite_send, above_send, below_send, lambda m: None)

    def make(q, m):
        extract(q, m)
        if ACROSS[m]:
            side_send(q, m)
        else:
            sends[q](m)

    def side_take(q, m):
        side_add(q, m)
        sends[q](m)

    def own(m):
        own_add(m)
        if ACROSS[m]:
            sub_send(m)
        else:
            side_send(3, m)

    def last(m):
        side_add(3, m)
        sub_send(m)

    steps = {"T": transforms, "E": make, "S": side_take, "A": above_pass, "B": below_pass, "O": own, "L": last}
    for name, *place_of in ORDER:
        steps[name](*place_of)

    start = starts_ref[s]
    within = start & 511
    shift, blocks = within & 127, within >> 7
    turned_window = window_ref[...]
    for bit in range(7):
        turned_window = jnp.where(
            ((shift >> bit) & 1) == 1, pltpu.roll(turned_window, 1 << bit, 1), turned_window
        )
    block_of, lane_of = iota((8, 128), 0), iota((8, 128), 1)
    taken = (block_of - blocks - jnp.where(lane_of < shift, 1, 0)) & 3
    weight = jnp.zeros((8, 128), F32)
    for b in range(4):
        weight = jnp.where(taken == b, jnp.broadcast_to(turned_window[b : b + 1, :], (8, 128)), weight)
    weight = jnp.concatenate([weight] * 4, axis=0)
    turns = ((iota((1, XM), 1) * within) & 511) * 32
    back_cos, back_sin = cos_turn(turns), cos_turn(turns - 4096)

    load_three.wait()
    got = landed.at[pl.ds(0, SUBS - 1)]
    pltpu.make_async_copy(got, got, sub_recv_sem).wait()
    for b in range(SUBS):
        scaled[pl.ds(b * 32, 32), :] = landed[b].astype(F32) * weight
    spectrum = jnp.concatenate(
        [
            jnp.concatenate([scaled[pl.ds(4 * h + i, 128, stride=8), :].astype(BF16) for i in range(4)], axis=1)
            for h in range(2)
        ],
        axis=0,
    )
    result = jnp.dot(spectrum, three[...], preferred_element_type=F32)
    re = result[:128, :XM] - result[128:, XM:]
    im = result[:128, XM:] + result[128:, :XM]
    for h, value in enumerate((re * back_cos + im * back_sin, im * back_cos - re * back_sin)):
        for b in range(SUBS):
            out_ref[h, b] = value[4 * b : 4 * b + 4, :]

    for copy in started:
        copy.wait_send()
    for m in range(GROUPS):
        own = s % GROUPS == m
        sent = parts.at[3, side, group(m)]

        @pl.when(own)
        def _():
            some = sent.at[pl.ds(0, ROWS - 32), :]
            pltpu.make_async_copy(some, some, sub_send_sem.at[m]).wait()

        @pl.when(jnp.logical_not(own))
        def _():
            pltpu.make_async_copy(sent, sent, sub_send_sem.at[m]).wait()


def local(image, correction, sizes, offsets, counts, lists, starts, window):
    out = pl.pallas_call(
        kernel,
        out_shape=jax.ShapeDtypeStruct((2, SUBS, 4, XM), F32),
        in_specs=[pl.BlockSpec(memory_space=pltpu.HBM)] * 10,
        out_specs=pl.BlockSpec(memory_space=pltpu.VMEM),
        scratch_shapes=[
            pltpu.VMEM((1, N), F32),
            pltpu.SMEM((1,), jnp.int32),
            pltpu.SMEM((1,), jnp.int32),
            pltpu.SMEM((1,), jnp.int32),
            pltpu.SMEM((SUBS,), jnp.int32),
            pltpu.VMEM((1, SUBS), jnp.int32),
            pltpu.VMEM((4, 128), F32),
            pltpu.VMEM((256, 128), BF16),
            pltpu.VMEM((KD, N), BF16),
            pltpu.VMEM((XM, 2 * XM), BF16),
            pltpu.VMEM((128 * KD, 128), F32),
            pltpu.VMEM((2, 256, 256), BF16),
            pltpu.VMEM((2, 2, 128, 128), F32),
            pltpu.VMEM((2, SUBS, 128), F32),
            pltpu.VMEM((4, 8, 128, 128), BF16),
            pltpu.VMEM((4, 8, 128, 128), BF16),
            pltpu.VMEM((4, 2, 4, 2, 32, 8, 128), F32),
            pltpu.VMEM((4, 2, SUBS * 32, 128), BF16),
            pltpu.VMEM((GROUPS, 4, ROWS, 128), BF16),
            pltpu.VMEM((GROUPS, ROWS, 128), BF16),
            pltpu.VMEM((GROUPS, ROWS, 128), BF16),
            pltpu.VMEM((GROUPS, 2, ROWS, 128), BF16),
            pltpu.VMEM((GROUPS, 2, ROWS, 128), BF16),
            pltpu.VMEM((SUBS, 32, 128), BF16),
            pltpu.VMEM((SUBS * 32, 128), F32),
            pltpu.SemaphoreType.DMA((8,)),
            pltpu.SemaphoreType.DMA((4,)),
            pltpu.SemaphoreType.DMA,
            pltpu.SemaphoreType.DMA((2, 3)),
            pltpu.SemaphoreType.DMA((2, 4)),
            pltpu.SemaphoreType.DMA((2, 4, GROUPS)),
            pltpu.SemaphoreType.DMA((2, 6, GROUPS)),
            pltpu.SemaphoreType.DMA((GROUPS,)),
            pltpu.SemaphoreType.DMA,
        ],
        compiler_params=pltpu.CompilerParams(
            collective_id=0, has_side_effects=True, vmem_limit_bytes=64 * 1024 * 1024
        ),
    )(
        image.reshape(KD, N), correction, sizes, offsets, counts, starts, lists, window.reshape(4, 128),
        jnp.asarray(table_one()), jnp.asarray(table_three()),
    )
    return out.reshape(1, 2, SUBS, 4, XM)


def solution(mesh):
    in_specs = (
        P("facet", "sub", None, None),
        P("facet", None),
        P("facet"),
        P("facet"),
        P("facet"),
        P("facet", None),
        P(),
        P(),
    )
    out_specs = P("sub", None, None, "facet", None)
    return jax.shard_map(local, mesh=mesh, in_specs=in_specs, out_specs=out_specs, check_vma=False)
```

```python
import functools
import math

import jax
import jax.numpy as jnp
import ml_dtypes
import numpy as np
from jax import lax
from jax.experimental import pallas as pl
from jax.experimental.pallas import tpu as pltpu
from jax.sharding import PartitionSpec as P

N = 16384
XM = 512
KD = 64
SUBS = 32
GROUPS = 8
PER = SUBS // GROUPS
ROWS = PER * 32
HALF = ROWS // 2
ACROSS = (True, False, True, False, True, False, False, False)
ORDER = (
    ("T", 0), ("E", 0, 3), ("E", 0, 0), ("E", 0, 4), ("E", 0, 7), ("E", 0, 2), ("E", 0, 6), ("E", 0, 5), ("E", 0, 1),
    ("T", 1), ("E", 1, 4), ("E", 1, 3), ("S", 0, 0), ("E", 1, 2), ("A", 3), ("E", 1, 0), ("S", 0, 4), ("T", 2),
    ("E", 2, 3), ("E", 2, 2), ("E", 2, 0), ("B", 3), ("E", 2, 1), ("E", 2, 4), ("S", 0, 2), ("B", 1), ("E", 1, 1),
    ("A", 1), ("T", 3), ("E", 3, 3), ("E", 3, 2), ("S", 1, 0), ("S", 2, 2), ("E", 3, 1), ("A", 0), ("O", 3),
    ("S", 2, 0), ("B", 0), ("E", 2, 5), ("B", 5), ("E", 3, 0), ("E", 1, 5), ("A", 5), ("B", 2), ("E", 3, 7),
    ("E", 3, 4), ("S", 1, 2), ("A", 2), ("E", 2, 6), ("S", 3, 2), ("O", 1), ("B", 6), ("S", 1, 4), ("A", 4),
    ("L", 3), ("E", 3, 5), ("E", 1, 6), ("A", 6), ("S", 2, 4), ("B", 4), ("E", 1, 7), ("S", 3, 0), ("O", 0),
    ("A", 7), ("E", 2, 7), ("S", 3, 4), ("B", 7), ("E", 3, 6), ("O", 5), ("L", 1), ("O", 2), ("L", 5), ("O", 6),
    ("O", 4), ("O", 7), ("L", 6), ("L", 7),
)
F32 = jnp.float32
BF16 = jnp.bfloat16
MESH = pl.DeviceIdType.MESH


def table_one():
    turns = np.outer(np.arange(128), np.arange(128)) % 128 * (2.0 * np.pi / 128)
    table = np.concatenate([np.cos(turns), -np.sin(turns)], axis=0) / math.sqrt(128.0)
    return table.astype(np.float32).astype(ml_dtypes.bfloat16)


def table_three():
    turns = np.outer(np.arange(XM), np.arange(XM)) % XM * (2.0 * np.pi / XM)
    table = np.concatenate([np.cos(turns), np.sin(turns)], axis=1) / math.sqrt(XM)
    return table.astype(np.float32).astype(ml_dtypes.bfloat16)


def cos_turn(index):
    index = index & (N - 1)
    quarter = (index + 2048) >> 12
    angle = (index - (quarter << 12)).astype(F32) * (2.0 * math.pi / N)
    square = angle * angle
    even = 1.0 + square * (-0.5 + square * (1 / 24 + square * (-1 / 720 + square * (1 / 40320))))
    odd = angle * (1.0 + square * (-1 / 6 + square * (1 / 120 + square * (-1 / 5040))))
    value = jnp.where((quarter & 1) == 1, odd, even)
    return jnp.where(((quarter + 1) & 2) == 2, -value, value)


def iota(shape, axis):
    return lax.broadcasted_iota(jnp.int32, shape, axis)


def add_to(target, *others):
    count = target.shape[0]
    size = max(size for size in (16, 32, 48, 64, 80, 96, 128) if count % size == 0)

    def body(i, carry):
        rows = pl.ds(pl.multiple_of(i * size, size), size)
        total = target[rows, :].astype(F32)
        for other in others:
            total = total + other[rows, :].astype(F32)
        target[rows, :] = total.astype(BF16)
        return carry

    lax.fori_loop(0, count // size, body, 0)


def kernel(
    image_hbm, gain_hbm, size_hbm, offset_hbm, count_hbm, starts_hbm, list_hbm, window_hbm, one_hbm, three_hbm,
    out_ref,
    gain_ref, size_ref, offset_ref, count_ref, starts_ref, list_ref, window_ref, one_ref,
    image, three, plane, two, turn, live, given, taken, spec, parts, side_in, up_in, down_in, up_two, down_two,
    landed, scaled,
    small_sem, image_sem, three_sem, table_sem, given_sem, side_sem, y_sem, sub_send_sem, sub_recv_sem,
):
    f, s = lax.axis_index("facet"), lax.axis_index("sub")
    core, side, y = f % 2, (f // 2) % 2, f // 4
    core_peer = f + 1 - 2 * core
    side_peer = f + 2 - 4 * side
    up = ((y + 1) % 4) * 4 + f % 4
    down = ((y + 3) % 4) * 4 + f % 4
    high, z = s // 16, s % 16
    taker = (side + high * (1 - 2 * side), side + (1 - high) * (1 - 2 * side))
    target = (f + high * (2 - 4 * side), f + (1 - high) * (2 - 4 * side))

    barrier = pltpu.get_barrier_semaphore()

    def greet(device):
        pl.semaphore_signal(barrier, inc=1, device_id=device, device_id_type=MESH)

    for step in range(16):
        there = (z + step) % 16
        greet({"facet": side_peer, "sub": (1 - high) * 16 + there})
        if step:
            greet({"sub": high * 16 + there})
    for peer in (core_peer, side_peer, up, down):
        greet({"facet": peer})

    small = [
        pltpu.make_async_copy(source, target, small_sem.at[i])
        for i, (source, target) in enumerate(
            (
                (offset_hbm, offset_ref), (count_hbm, count_ref), (list_hbm, list_ref), (size_hbm, size_ref), (gain_hbm, gain_ref), (one_hbm, one_ref),
                (starts_hbm, starts_ref), (window_hbm, window_ref),
            )
        )
    ]
    for load in small:
        load.start()
    loads = [
        pltpu.make_async_copy(
            image_hbm.at[:, pl.ds(part * 4096, 4096)], image.at[:, pl.ds(part * 4096, 4096)], image_sem.at[part]
        )
        for part in range(4)
    ]
    for load in loads:
        load.start()
    load_three = pltpu.make_async_copy(three_hbm, three, three_sem)
    load_three.start()

    for load in small:
        load.wait()
    offset = offset_ref[0] & (N - 1)
    row, lane = iota((256, 256), 0), iota((256, 256), 1)
    freq = (row >> 3) * 4 + (row & 3)
    turns = freq * ((lane & 127) + offset) * 128 + 4096 * (((row >> 2) & 1) - (lane >> 7))
    two[0] = (cos_turn(turns) * (1.0 / math.sqrt(128.0))).astype(BF16)
    turns = iota((128, 128), 0) * (iota((128, 128), 1) + offset)
    turn[0, 0] = cos_turn(turns)
    turn[0, 1] = cos_turn(turns - 4096)
    named = (list_ref[...] == iota((SUBS, SUBS), 0)) & (iota((SUBS, SUBS), 1) < count_ref[0])
    live[0] = jnp.broadcast_to(jnp.sum(jnp.where(named, 1.0, 0.0), axis=1, keepdims=True), (SUBS, 128))

    started = []

    def go(source, target, send, recv, device):
        copy = pltpu.make_async_remote_copy(
            src_ref=source, dst_ref=target, send_sem=send, recv_sem=recv, device_id=device, device_id_type=MESH
        )
        copy.start()
        started.append(copy)
        return copy

    size = size_ref[0]

    def fill(a, carry):
        first = pl.multiple_of(a * 128, 128)
        gain = jnp.where(iota((1, 128), 1) + first < size, gain_ref[:, pl.ds(first, 128)], 0.0)
        plane[pl.ds(pl.multiple_of(a * KD, KD), KD), :] = image[:, pl.ds(first, 128)].astype(F32) * gain
        return carry

    for part in range(4):
        loads[part].wait()
        lax.fori_loop(part * 32, part * 32 + 32, fill, 0, unroll=2)

    block_y = ((y + 2) % 4, (y + 1) % 4, (y + 3) % 4, y)

    for q in range(4):
        for x in range(2):
            for j in range(4):
                column = 16 * block_y[q] + 8 * x + 4 * (1 - core) + j
                given[q, 4 * x + j] = plane[pl.ds(column, 128, stride=KD), :].astype(BF16)

    pl.semaphore_wait(barrier, SUBS + 3)
    tables = [
        go(table.at[0], table.at[1], table_sem.at[0, i], table_sem.at[1, i], {"facet": core_peer})
        for i, table in enumerate((two, turn, live))
    ]

    gifts = [
        go(given.at[q], taken.at[q], given_sem.at[0, q], given_sem.at[1, q], {"facet": core_peer}) for q in range(4)
    ]

    def transform(q, source, pair):
        if source == 0:
            first = 16 * block_y[q] + 8 * (pair // 2) + 4 * core + 2 * (pair % 2)
            columns = [plane[pl.ds(first + j, 128, stride=KD), :].astype(BF16) for j in range(2)]
        else:
            columns = [taken[q, 2 * pair + j] for j in range(2)]
        section = jnp.dot(one_ref[...], jnp.concatenate(columns, axis=1), preferred_element_type=F32)
        turned = []
        for j in range(2):
            re, im = section[:128, j * 128 : j * 128 + 128], section[128:, j * 128 : j * 128 + 128]
            cosine, sine = turn[source, 0], turn[source, 1]
            turned.append(
                jnp.concatenate([re * cosine + im * sine, im * cosine - re * sine], axis=1).astype(BF16)
            )
        result = lax.dot_general(
            two[source], jnp.concatenate(turned, axis=0), (((1,), (1,)), ((), ())), preferred_element_type=F32
        )
        for j in range(2):
            spec[q, source, pair, j] = result[:, j * 128 : j * 128 + 128].reshape(32, 8, 128)

    def transforms(q):
        if q > 0:
            gifts[q].wait_recv()
        for pair in range(4):
            transform(q, 0, pair)
        if q == 0:
            for table in tables:
                table.wait_recv()
            gifts[q].wait_recv()
        for pair in range(4):
            transform(q, 1, pair)

    place = (iota((8, 128), 0) & 3) * 128 + iota((8, 128), 1)

    def extract(q, m):
        def body(i, carry):
            g = i * GROUPS + m
            start = starts_ref[g]
            low = (start >> 9) & 31
            high = (low + 1) & 31
            inside = place >= (start & 511)
            weights = [jnp.broadcast_to(live[source, pl.ds(g, 1), :], (8, 128)) for source in range(2)]
            for pair in range(4):
                tiles = []
                for j in range(2):
                    windows = [
                        jnp.where(inside, spec[q, source, pair, j, low], spec[q, source, pair, j, high])
                        for source in range(2)
                    ]
                    tiles.append(windows[0] * weights[0] + windows[1] * weights[1])
                rows = pl.ds(pl.multiple_of(m * ROWS + i * 32 + (pair % 2) * 16, 16), 16)
                parts[q, pair // 2, rows, :] = jnp.concatenate(tiles, axis=0).astype(BF16)
            return carry

        lax.fori_loop(0, PER, body, 0, unroll=2)

    copies = {}

    def group(m):
        return pl.ds(m * ROWS, ROWS)

    def half_of(m, h):
        return pl.ds(m * ROWS + h * HALF, HALF)

    def side_send(q, m):
        for h in range(2):
            copies["side", q, m, h] = go(
                parts.at[q, 1 - taker[h], half_of(m, h)], side_in.at[m, q, pl.ds(h * HALF, HALF)],
                side_sem.at[0, q, m, h], side_sem.at[1, q, m, h], {"facet": side_peer},
            )

    def side_add(q, m):
        for h in range(2):
            copies["side", q, m, h].wait_recv()
            add_to(parts.at[q, taker[h], half_of(m, h)], side_in.at[m, q, pl.ds(h * HALF, HALF)])

    def piece(q, m, p):
        if ACROSS[m]:
            return parts.at[q, taker[p], half_of(m, p)]
        return parts.at[q, p, group(m)]

    size_of = [pl.ds(0, HALF if across else ROWS) for across in ACROSS]

    def along_y(number, q, m, p, target, peer):
        copies["y", number, m] = go(
            piece(q, m, p), target, y_sem.at[0, number, m], y_sem.at[1, number, m], {"facet": peer}
        )

    def opposite_send(m):
        along_y(0, 0, m, 0, up_in.at[m, size_of[m]], up)
        along_y(1, 0, m, 1, down_in.at[m, size_of[m]], down)

    def above_send(m):
        along_y(2, 1, m, 1, up_two.at[m, 1, size_of[m]], up)

    def above_pass(m):
        copies["y", 0, m].wait_recv()
        add_to(piece(1, m, 0), up_in.at[m, size_of[m]])
        along_y(3, 1, m, 0, up_two.at[m, 0, size_of[m]], up)

    def below_send(m):
        along_y(4, 2, m, 0, down_two.at[m, 0, size_of[m]], down)

    def below_pass(m):
        copies["y", 1, m].wait_recv()
        add_to(piece(2, m, 1), down_in.at[m, size_of[m]])
        along_y(5, 2, m, 1, down_two.at[m, 1, size_of[m]], down)

    def own_add(m):
        for number in range(2, 6):
            copies["y", number, m].wait_recv()
        for p in range(2):
            add_to(piece(3, m, p), up_two.at[m, p, size_of[m]], down_two.at[m, p, size_of[m]])

    def sub_send(m):
        home = z // GROUPS
        count = PER // 2
        for step in sorted(range(count), key=lambda d: -min(d, count - d)):
            i = (home + step) % count
            for h in range(2):
                row = m * ROWS + h * HALF + i * 32
                block = parts.at[3, taker[h], pl.ds(pl.multiple_of(row, 32), 32), :]
                copy = pltpu.make_async_remote_copy(
                    src_ref=block, dst_ref=landed.at[s], send_sem=sub_send_sem.at[m], recv_sem=sub_recv_sem,
                    device_id={"facet": target[h], "sub": h * 16 + i * GROUPS + m}, device_id_type=MESH,
                )
                if step:
                    copy.start()
                else:
                    own = jnp.logical_and(high == h, z % GROUPS == m)

                    @pl.when(own)
                    def _():
                        landed[s] = block[...]

                    @pl.when(jnp.logical_not(own))
                    def _():
                        copy.start()

    sends = (opposite_send, above_send, below_send, lambda m: None)

    def make(q, m):
        extract(q, m)
        if ACROSS[m]:
            side_send(q, m)
        else:
            sends[q](m)

    def side_take(q, m):
        side_add(q, m)
        sends[q](m)

    def own(m):
        own_add(m)
        if ACROSS[m]:
            sub_send(m)
        else:
            side_send(3, m)

    def last(m):
        side_add(3, m)
        sub_send(m)

    steps = {"T": transforms, "E": make, "S": side_take, "A": above_pass, "B": below_pass, "O": own, "L": last}
    for name, *place_of in ORDER:
        steps[name](*place_of)

    start = starts_ref[s]
    within = start & 511
    shift, blocks = within & 127, within >> 7
    turned_window = window_ref[...]
    for bit in range(7):
        turned_window = jnp.where(
            ((shift >> bit) & 1) == 1, pltpu.roll(turned_window, 1 << bit, 1), turned_window
        )
    block_of, lane_of = iota((8, 128), 0), iota((8, 128), 1)
    taken = (block_of - blocks - jnp.where(lane_of < shift, 1, 0)) & 3
    weight = jnp.zeros((8, 128), F32)
    for b in range(4):
        weight = jnp.where(taken == b, jnp.broadcast_to(turned_window[b : b + 1, :], (8, 128)), weight)
    weight = jnp.concatenate([weight] * 4, axis=0)
    turns = ((iota((1, XM), 1) * within) & 511) * 32
    back_cos, back_sin = cos_turn(turns), cos_turn(turns - 4096)

    load_three.wait()
    got = landed.at[pl.ds(0, SUBS - 1)]
    pltpu.make_async_copy(got, got, sub_recv_sem).wait()
    for b in range(SUBS):
        scaled[pl.ds(b * 32, 32), :] = landed[b].astype(F32) * weight
    spectrum = jnp.concatenate(
        [
            jnp.concatenate([scaled[pl.ds(4 * h + i, 128, stride=8), :].astype(BF16) for i in range(4)], axis=1)
            for h in range(2)
        ],
        axis=0,
    )
    result = jnp.dot(spectrum, three[...], preferred_element_type=F32)
    re = result[:128, :XM] - result[128:, XM:]
    im = result[:128, XM:] + result[128:, :XM]
    for h, value in enumerate((re * back_cos + im * back_sin, im * back_cos - re * back_sin)):
        for b in range(SUBS):
            out_ref[h, b] = value[4 * b : 4 * b + 4, :]

    for copy in started:
        copy.wait_send()
    for m in range(GROUPS):
        own = z % GROUPS == m
        sent = parts.at[3, 0, group(m)]

        @pl.when(own)
        def _():
            some = sent.at[pl.ds(0, ROWS - 32), :]
            pltpu.make_async_copy(some, some, sub_send_sem.at[m]).wait()

        @pl.when(jnp.logical_not(own))
        def _():
            pltpu.make_async_copy(sent, sent, sub_send_sem.at[m]).wait()


def local(image, correction, sizes, offsets, counts, lists, starts, window):
    out = pl.pallas_call(
        kernel,
        out_shape=jax.ShapeDtypeStruct((2, SUBS, 4, XM), F32),
        in_specs=[pl.BlockSpec(memory_space=pltpu.HBM)] * 10,
        out_specs=pl.BlockSpec(memory_space=pltpu.VMEM),
        scratch_shapes=[
            pltpu.VMEM((1, N), F32),
            pltpu.SMEM((1,), jnp.int32),
            pltpu.SMEM((1,), jnp.int32),
            pltpu.SMEM((1,), jnp.int32),
            pltpu.SMEM((SUBS,), jnp.int32),
            pltpu.VMEM((1, SUBS), jnp.int32),
            pltpu.VMEM((4, 128), F32),
            pltpu.VMEM((256, 128), BF16),
            pltpu.VMEM((KD, N), BF16),
            pltpu.VMEM((XM, 2 * XM), BF16),
            pltpu.VMEM((128 * KD, 128), F32),
            pltpu.VMEM((2, 256, 256), BF16),
            pltpu.VMEM((2, 2, 128, 128), F32),
            pltpu.VMEM((2, SUBS, 128), F32),
            pltpu.VMEM((4, 8, 128, 128), BF16),
            pltpu.VMEM((4, 8, 128, 128), BF16),
            pltpu.VMEM((4, 2, 4, 2, 32, 8, 128), F32),
            pltpu.VMEM((4, 2, SUBS * 32, 128), BF16),
            pltpu.VMEM((GROUPS, 4, ROWS, 128), BF16),
            pltpu.VMEM((GROUPS, ROWS, 128), BF16),
            pltpu.VMEM((GROUPS, ROWS, 128), BF16),
            pltpu.VMEM((GROUPS, 2, ROWS, 128), BF16),
            pltpu.VMEM((GROUPS, 2, ROWS, 128), BF16),
            pltpu.VMEM((SUBS, 32, 128), BF16),
            pltpu.VMEM((SUBS * 32, 128), F32),
            pltpu.SemaphoreType.DMA((8,)),
            pltpu.SemaphoreType.DMA((4,)),
            pltpu.SemaphoreType.DMA,
            pltpu.SemaphoreType.DMA((2, 3)),
            pltpu.SemaphoreType.DMA((2, 4)),
            pltpu.SemaphoreType.DMA((2, 4, GROUPS, 2)),
            pltpu.SemaphoreType.DMA((2, 6, GROUPS)),
            pltpu.SemaphoreType.DMA((GROUPS,)),
            pltpu.SemaphoreType.DMA,
        ],
        compiler_params=pltpu.CompilerParams(
            collective_id=0, has_side_effects=True, vmem_limit_bytes=64 * 1024 * 1024
        ),
    )(
        image.reshape(KD, N), correction, sizes, offsets, counts, starts, lists, window.reshape(4, 128),
        jnp.asarray(table_one()), jnp.asarray(table_three()),
    )
    return out.reshape(1, 2, SUBS, 4, XM)


def solution(mesh):
    in_specs = (
        P("facet", "sub", None, None),
        P("facet", None),
        P("facet"),
        P("facet"),
        P("facet"),
        P("facet", None),
        P(),
        P(),
    )
    out_specs = P("sub", None, None, "facet", None)
    return jax.shard_map(local, mesh=mesh, in_specs=in_specs, out_specs=out_specs, check_vma=False)
```

```python
import functools
import math

import jax
import jax.numpy as jnp
import ml_dtypes
import numpy as np
from jax import lax
from jax.experimental import pallas as pl
from jax.experimental.pallas import tpu as pltpu
from jax.sharding import PartitionSpec as P

N = 16384
XM = 512
KD = 64
SUBS = 32
GROUPS = 8
PER = SUBS // GROUPS
ROWS = PER * 32
HALF = ROWS // 2
ACROSS = (True, False, True, False, True, False, False, False)
ORDER = (
    ("T", 0), ("E", 0, 3), ("E", 0, 0), ("E", 0, 4), ("E", 0, 7), ("E", 0, 2), ("E", 0, 6), ("E", 0, 5), ("E", 0, 1),
    ("T", 1), ("E", 1, 4), ("E", 1, 3), ("S", 0, 0), ("E", 1, 2), ("A", 3), ("E", 1, 0), ("S", 0, 4), ("T", 2),
    ("E", 2, 3), ("E", 2, 2), ("E", 2, 0), ("B", 3), ("E", 2, 1), ("E", 2, 4), ("S", 0, 2), ("B", 1), ("E", 1, 1),
    ("A", 1), ("T", 3), ("E", 3, 3), ("E", 3, 2), ("S", 1, 0), ("S", 2, 2), ("E", 3, 1), ("A", 0), ("O", 3),
    ("S", 2, 0), ("B", 0), ("E", 2, 5), ("B", 5), ("E", 3, 0), ("E", 1, 5), ("A", 5), ("B", 2), ("E", 3, 7),
    ("E", 3, 4), ("S", 1, 2), ("A", 2), ("E", 2, 6), ("S", 3, 2), ("O", 1), ("B", 6), ("S", 1, 4), ("A", 4),
    ("L", 3), ("E", 3, 5), ("E", 1, 6), ("A", 6), ("S", 2, 4), ("B", 4), ("E", 1, 7), ("S", 3, 0), ("O", 0),
    ("A", 7), ("E", 2, 7), ("S", 3, 4), ("B", 7), ("E", 3, 6), ("O", 5), ("L", 1), ("O", 2), ("L", 5), ("O", 6),
    ("O", 4), ("O", 7), ("L", 6), ("L", 7),
)
F32 = jnp.float32
BF16 = jnp.bfloat16
MESH = pl.DeviceIdType.MESH


def table_one():
    turns = np.outer(np.arange(128), np.arange(128)) % 128 * (2.0 * np.pi / 128)
    table = np.concatenate([np.cos(turns), -np.sin(turns)], axis=0) / math.sqrt(128.0)
    return table.astype(np.float32).astype(ml_dtypes.bfloat16)


def table_three():
    turns = np.outer(np.arange(XM), np.arange(XM)) % XM * (2.0 * np.pi / XM)
    table = np.concatenate([np.cos(turns), np.sin(turns)], axis=1) / math.sqrt(XM)
    return table.astype(np.float32).astype(ml_dtypes.bfloat16)


def cos_turn(index):
    index = index & (N - 1)
    quarter = (index + 2048) >> 12
    angle = (index - (quarter << 12)).astype(F32) * (2.0 * math.pi / N)
    square = angle * angle
    even = 1.0 + square * (-0.5 + square * (1 / 24 + square * (-1 / 720 + square * (1 / 40320))))
    odd = angle * (1.0 + square * (-1 / 6 + square * (1 / 120 + square * (-1 / 5040))))
    value = jnp.where((quarter & 1) == 1, odd, even)
    return jnp.where(((quarter + 1) & 2) == 2, -value, value)


def iota(shape, axis):
    return lax.broadcasted_iota(jnp.int32, shape, axis)


def add_to(target, *others):
    count = target.shape[0]
    size = max(size for size in (16, 32, 48, 64, 80, 96, 128) if count % size == 0)

    def body(i, carry):
        rows = pl.ds(pl.multiple_of(i * size, size), size)
        total = target[rows, :].astype(F32)
        for other in others:
            total = total + other[rows, :].astype(F32)
        target[rows, :] = total.astype(BF16)
        return carry

    lax.fori_loop(0, count // size, body, 0)


def kernel(
    image_hbm, gain_hbm, size_hbm, offset_hbm, count_hbm, starts_hbm, list_hbm, window_hbm, one_hbm, three_hbm,
    out_ref,
    gain_ref, size_ref, offset_ref, count_ref, starts_ref, list_ref, window_ref, one_ref,
    image, three, plane, two, turn, live, given, taken, spec, parts, side_in, up_in, down_in, up_two, down_two,
    landed, scaled,
    small_sem, image_sem, three_sem, table_sem, given_sem, side_sem, y_sem, sub_send_sem, sub_recv_sem,
):
    f, s = lax.axis_index("facet"), lax.axis_index("sub")
    core, side, y = f % 2, (f // 2) % 2, f // 4
    core_peer = f + 1 - 2 * core
    side_peer = f + 2 - 4 * side
    up = ((y + 1) % 4) * 4 + f % 4
    down = ((y + 3) % 4) * 4 + f % 4
    high, z = s // 16, s % 16
    taker = (side + high * (1 - 2 * side), side + (1 - high) * (1 - 2 * side))
    target = (f + high * (2 - 4 * side), f + (1 - high) * (2 - 4 * side))

    barrier = pltpu.get_barrier_semaphore()

    def greet(device):
        pl.semaphore_signal(barrier, inc=1, device_id=device, device_id_type=MESH)

    for step in range(16):
        there = (z + step) % 16
        greet({"facet": side_peer, "sub": (1 - high) * 16 + there})
        if step:
            greet({"sub": high * 16 + there})
    for peer in (core_peer, side_peer, up, down):
        greet({"facet": peer})

    small = [
        pltpu.make_async_copy(source, target, small_sem.at[i])
        for i, (source, target) in enumerate(
            (
                (offset_hbm, offset_ref), (count_hbm, count_ref), (list_hbm, list_ref), (size_hbm, size_ref), (gain_hbm, gain_ref), (one_hbm, one_ref),
                (starts_hbm, starts_ref), (window_hbm, window_ref),
            )
        )
    ]
    for load in small:
        load.start()
    loads = [
        pltpu.make_async_copy(
            image_hbm.at[:, pl.ds(part * 4096, 4096)], image.at[:, pl.ds(part * 4096, 4096)], image_sem.at[part]
        )
        for part in range(4)
    ]
    for load in loads:
        load.start()
    load_three = pltpu.make_async_copy(three_hbm, three, three_sem)
    load_three.start()

    for load in small:
        load.wait()
    offset = offset_ref[0] & (N - 1)
    row, lane = iota((256, 256), 0), iota((256, 256), 1)
    freq = (row >> 3) * 4 + (row & 3)
    turns = freq * ((lane & 127) + offset) * 128 + 4096 * (((row >> 2) & 1) - (lane >> 7))
    two[0] = (cos_turn(turns) * (1.0 / math.sqrt(128.0))).astype(BF16)
    turns = iota((128, 128), 0) * (iota((128, 128), 1) + offset)
    turn[0, 0] = cos_turn(turns)
    turn[0, 1] = cos_turn(turns - 4096)
    named = (list_ref[...] == iota((SUBS, SUBS), 0)) & (iota((SUBS, SUBS), 1) < count_ref[0])
    live[0] = jnp.broadcast_to(jnp.sum(jnp.where(named, 1.0, 0.0), axis=1, keepdims=True), (SUBS, 128))

    started = []

    def go(source, target, send, recv, device):
        copy = pltpu.make_async_remote_copy(
            src_ref=source, dst_ref=target, send_sem=send, recv_sem=recv, device_id=device, device_id_type=MESH
        )
        copy.start()
        started.append(copy)
        return copy

    size = size_ref[0]

    def fill(a, carry):
        first = pl.multiple_of(a * 128, 128)
        gain = jnp.where(iota((1, 128), 1) + first < size, gain_ref[:, pl.ds(first, 128)], 0.0)
        plane[pl.ds(pl.multiple_of(a * KD, KD), KD), :] = image[:, pl.ds(first, 128)].astype(F32) * gain
        return carry

    for part in range(4):
        loads[part].wait()
        lax.fori_loop(part * 32, part * 32 + 32, fill, 0, unroll=2)

    block_y = ((y + 2) % 4, (y + 1) % 4, (y + 3) % 4, y)

    for q in range(4):
        for x in range(2):
            for j in range(4):
                column = 16 * block_y[q] + 8 * x + 4 * (1 - core) + j
                given[q, 4 * x + j] = plane[pl.ds(column, 128, stride=KD), :].astype(BF16)

    pl.semaphore_wait(barrier, SUBS + 3)
    tables = [
        go(table.at[0], table.at[1], table_sem.at[0, i], table_sem.at[1, i], {"facet": core_peer})
        for i, table in enumerate((two, turn, live))
    ]

    gifts = [
        go(given.at[q], taken.at[q], given_sem.at[0, q], given_sem.at[1, q], {"facet": core_peer}) for q in range(4)
    ]

    def transform(q, source, pair):
        if source == 0:
            first = 16 * block_y[q] + 8 * (pair // 2) + 4 * core + 2 * (pair % 2)
            columns = [plane[pl.ds(first + j, 128, stride=KD), :].astype(BF16) for j in range(2)]
        else:
            columns = [taken[q, 2 * pair + j] for j in range(2)]
        section = jnp.dot(one_ref[...], jnp.concatenate(columns, axis=1), preferred_element_type=F32)
        turned = []
        for j in range(2):
            re, im = section[:128, j * 128 : j * 128 + 128], section[128:, j * 128 : j * 128 + 128]
            cosine, sine = turn[source, 0], turn[source, 1]
            turned.append(
                jnp.concatenate([re * cosine + im * sine, im * cosine - re * sine], axis=1).astype(BF16)
            )
        result = lax.dot_general(
            two[source], jnp.concatenate(turned, axis=0), (((1,), (1,)), ((), ())), preferred_element_type=F32
        )
        for j in range(2):
            spec[q, source, pair, j] = result[:, j * 128 : j * 128 + 128].reshape(32, 8, 128)

    def transforms(q):
        if q > 1:
            gifts[q].wait_recv()
        for block in ((0, 1), (), (2,), (3,))[q]:
            for pair in range(4):
                transform(block, 0, pair)
        if q == 0:
            for table in tables:
                table.wait_recv()
        if q < 2:
            gifts[q].wait_recv()
        for pair in range(4):
            transform(q, 1, pair)

    place = (iota((8, 128), 0) & 3) * 128 + iota((8, 128), 1)

    def extract(q, m):
        def body(i, carry):
            g = i * GROUPS + m
            start = starts_ref[g]
            low = (start >> 9) & 31
            high = (low + 1) & 31
            inside = place >= (start & 511)
            weights = [jnp.broadcast_to(live[source, pl.ds(g, 1), :], (8, 128)) for source in range(2)]
            for pair in range(4):
                tiles = []
                for j in range(2):
                    windows = [
                        jnp.where(inside, spec[q, source, pair, j, low], spec[q, source, pair, j, high])
                        for source in range(2)
                    ]
                    tiles.append(windows[0] * weights[0] + windows[1] * weights[1])
                rows = pl.ds(pl.multiple_of(m * ROWS + i * 32 + (pair % 2) * 16, 16), 16)
                parts[q, pair // 2, rows, :] = jnp.concatenate(tiles, axis=0).astype(BF16)
            return carry

        lax.fori_loop(0, PER, body, 0, unroll=2)

    copies = {}

    def group(m):
        return pl.ds(m * ROWS, ROWS)

    def half_of(m, h):
        return pl.ds(m * ROWS + h * HALF, HALF)

    def side_send(q, m):
        for h in range(2):
            copies["side", q, m, h] = go(
                parts.at[q, 1 - taker[h], half_of(m, h)], side_in.at[m, q, pl.ds(h * HALF, HALF)],
                side_sem.at[0, q, m, h], side_sem.at[1, q, m, h], {"facet": side_peer},
            )

    def side_add(q, m):
        for h in range(2):
            copies["side", q, m, h].wait_recv()
            add_to(parts.at[q, taker[h], half_of(m, h)], side_in.at[m, q, pl.ds(h * HALF, HALF)])

    def piece(q, m, p):
        if ACROSS[m]:
            return parts.at[q, taker[p], half_of(m, p)]
        return parts.at[q, p, group(m)]

    size_of = [pl.ds(0, HALF if across else ROWS) for across in ACROSS]

    def along_y(number, q, m, p, target, peer):
        copies["y", number, m] = go(
            piece(q, m, p), target, y_sem.at[0, number, m], y_sem.at[1, number, m], {"facet": peer}
        )

    def opposite_send(m):
        along_y(0, 0, m, 0, up_in.at[m, size_of[m]], up)
        along_y(1, 0, m, 1, down_in.at[m, size_of[m]], down)

    def above_send(m):
        along_y(2, 1, m, 1, up_two.at[m, 1, size_of[m]], up)

    def above_pass(m):
        copies["y", 0, m].wait_recv()
        add_to(piece(1, m, 0), up_in.at[m, size_of[m]])
        along_y(3, 1, m, 0, up_two.at[m, 0, size_of[m]], up)

    def below_send(m):
        along_y(4, 2, m, 0, down_two.at[m, 0, size_of[m]], down)

    def below_pass(m):
        copies["y", 1, m].wait_recv()
        add_to(piece(2, m, 1), down_in.at[m, size_of[m]])
        along_y(5, 2, m, 1, down_two.at[m, 1, size_of[m]], down)

    def own_add(m):
        for number in range(2, 6):
            copies["y", number, m].wait_recv()
        for p in range(2):
            add_to(piece(3, m, p), up_two.at[m, p, size_of[m]], down_two.at[m, p, size_of[m]])

    def sub_send(m):
        home = z // GROUPS
        count = PER // 2
        for step in sorted(range(count), key=lambda d: -min(d, count - d)):
            i = (home + step) % count
            for h in range(2):
                row = m * ROWS + h * HALF + i * 32
                block = parts.at[3, taker[h], pl.ds(pl.multiple_of(row, 32), 32), :]
                copy = pltpu.make_async_remote_copy(
                    src_ref=block, dst_ref=landed.at[s], send_sem=sub_send_sem.at[m], recv_sem=sub_recv_sem,
                    device_id={"facet": target[h], "sub": h * 16 + i * GROUPS + m}, device_id_type=MESH,
                )
                if step:
                    copy.start()
                else:
                    own = jnp.logical_and(high == h, z % GROUPS == m)

                    @pl.when(own)
                    def _():
                        landed[s] = block[...]

                    @pl.when(jnp.logical_not(own))
                    def _():
                        copy.start()

    sends = (opposite_send, above_send, below_send, lambda m: None)

    def make(q, m):
        extract(q, m)
        if ACROSS[m]:
            side_send(q, m)
        else:
            sends[q](m)

    def side_take(q, m):
        side_add(q, m)
        sends[q](m)

    def own(m):
        own_add(m)
        if ACROSS[m]:
            sub_send(m)
        else:
            side_send(3, m)

    def last(m):
        side_add(3, m)
        sub_send(m)

    steps = {"T": transforms, "E": make, "S": side_take, "A": above_pass, "B": below_pass, "O": own, "L": last}
    for name, *place_of in ORDER:
        steps[name](*place_of)

    start = starts_ref[s]
    within = start & 511
    shift, blocks = within & 127, within >> 7
    turned_window = window_ref[...]
    for bit in range(7):
        turned_window = jnp.where(
            ((shift >> bit) & 1) == 1, pltpu.roll(turned_window, 1 << bit, 1), turned_window
        )
    block_of, lane_of = iota((8, 128), 0), iota((8, 128), 1)
    taken = (block_of - blocks - jnp.where(lane_of < shift, 1, 0)) & 3
    weight = jnp.zeros((8, 128), F32)
    for b in range(4):
        weight = jnp.where(taken == b, jnp.broadcast_to(turned_window[b : b + 1, :], (8, 128)), weight)
    weight = jnp.concatenate([weight] * 4, axis=0)
    turns = ((iota((1, XM), 1) * within) & 511) * 32
    back_cos, back_sin = cos_turn(turns), cos_turn(turns - 4096)

    load_three.wait()
    got = landed.at[pl.ds(0, SUBS - 1)]
    pltpu.make_async_copy(got, got, sub_recv_sem).wait()
    for b in range(SUBS):
        scaled[pl.ds(b * 32, 32), :] = landed[b].astype(F32) * weight
    spectrum = jnp.concatenate(
        [
            jnp.concatenate([scaled[pl.ds(4 * h + i, 128, stride=8), :].astype(BF16) for i in range(4)], axis=1)
            for h in range(2)
        ],
        axis=0,
    )
    result = jnp.dot(spectrum, three[...], preferred_element_type=F32)
    re = result[:128, :XM] - result[128:, XM:]
    im = result[:128, XM:] + result[128:, :XM]
    for h, value in enumerate((re * back_cos + im * back_sin, im * back_cos - re * back_sin)):
        for b in range(SUBS):
            out_ref[h, b] = value[4 * b : 4 * b + 4, :]

    for copy in started:
        copy.wait_send()
    for m in range(GROUPS):
        own = z % GROUPS == m
        sent = parts.at[3, 0, group(m)]

        @pl.when(own)
        def _():
            some = sent.at[pl.ds(0, ROWS - 32), :]
            pltpu.make_async_copy(some, some, sub_send_sem.at[m]).wait()

        @pl.when(jnp.logical_not(own))
        def _():
            pltpu.make_async_copy(sent, sent, sub_send_sem.at[m]).wait()


def local(image, correction, sizes, offsets, counts, lists, starts, window):
    out = pl.pallas_call(
        kernel,
        out_shape=jax.ShapeDtypeStruct((2, SUBS, 4, XM), F32),
        in_specs=[pl.BlockSpec(memory_space=pltpu.HBM)] * 10,
        out_specs=pl.BlockSpec(memory_space=pltpu.VMEM),
        scratch_shapes=[
            pltpu.VMEM((1, N), F32),
            pltpu.SMEM((1,), jnp.int32),
            pltpu.SMEM((1,), jnp.int32),
            pltpu.SMEM((1,), jnp.int32),
            pltpu.SMEM((SUBS,), jnp.int32),
            pltpu.VMEM((1, SUBS), jnp.int32),
            pltpu.VMEM((4, 128), F32),
            pltpu.VMEM((256, 128), BF16),
            pltpu.VMEM((KD, N), BF16),
            pltpu.VMEM((XM, 2 * XM), BF16),
            pltpu.VMEM((128 * KD, 128), F32),
            pltpu.VMEM((2, 256, 256), BF16),
            pltpu.VMEM((2, 2, 128, 128), F32),
            pltpu.VMEM((2, SUBS, 128), F32),
            pltpu.VMEM((4, 8, 128, 128), BF16),
            pltpu.VMEM((4, 8, 128, 128), BF16),
            pltpu.VMEM((4, 2, 4, 2, 32, 8, 128), F32),
            pltpu.VMEM((4, 2, SUBS * 32, 128), BF16),
            pltpu.VMEM((GROUPS, 4, ROWS, 128), BF16),
            pltpu.VMEM((GROUPS, ROWS, 128), BF16),
            pltpu.VMEM((GROUPS, ROWS, 128), BF16),
            pltpu.VMEM((GROUPS, 2, ROWS, 128), BF16),
            pltpu.VMEM((GROUPS, 2, ROWS, 128), BF16),
            pltpu.VMEM((SUBS, 32, 128), BF16),
            pltpu.VMEM((SUBS * 32, 128), F32),
            pltpu.SemaphoreType.DMA((8,)),
            pltpu.SemaphoreType.DMA((4,)),
            pltpu.SemaphoreType.DMA,
            pltpu.SemaphoreType.DMA((2, 3)),
            pltpu.SemaphoreType.DMA((2, 4)),
            pltpu.SemaphoreType.DMA((2, 4, GROUPS, 2)),
            pltpu.SemaphoreType.DMA((2, 6, GROUPS)),
            pltpu.SemaphoreType.DMA((GROUPS,)),
            pltpu.SemaphoreType.DMA,
        ],
        compiler_params=pltpu.CompilerParams(
            collective_id=0, has_side_effects=True, vmem_limit_bytes=64 * 1024 * 1024
        ),
    )(
        image.reshape(KD, N), correction, sizes, offsets, counts, starts, lists, window.reshape(4, 128),
        jnp.asarray(table_one()), jnp.asarray(table_three()),
    )
    return out.reshape(1, 2, SUBS, 4, XM)


def solution(mesh):
    in_specs = (
        P("facet", "sub", None, None),
        P("facet", None),
        P("facet"),
        P("facet"),
        P("facet"),
        P("facet", None),
        P(),
        P(),
    )
    out_specs = P("sub", None, None, "facet", None)
    return jax.shard_map(local, mesh=mesh, in_specs=in_specs, out_specs=out_specs, check_vma=False)
```
